256 devices in a mesh: dp: 8 (over x, core), fsdp: 32 (over y, z).
Axes of the slice: x: 4, y: 4, z: 8, core: 2. Of those that a mesh axis runs over, the one named last changes fastest.
Arguments:
- grad_parts: bfloat16 [8, 8, 1024, 1024], P(None, 'dp', 'fsdp'), may hold values from -0.875 to 0.875
- first_moment: float32 [8, 1024, 1024], P('dp', 'fsdp'), may hold values from -1.5 to 1.5
- second_moment: float32 [8, 1024, 1024], P('dp', 'fsdp'), may hold values from 0.002 to 0.02
- left_gram: float32 [8, 1024, 1024], P('dp', 'fsdp'), may hold values from -1 to 4
- right_gram: float32 [8, 1024, 1024], P('dp', 'fsdp'), may hold values from -1 to 4
- left_basis: float32 [8, 1024, 1024], P('dp', 'fsdp'), may hold values from -1 to 2
- right_basis: float32 [8, 1024, 1024], P('dp', 'fsdp'), may hold values from -1 to 2
- due_flags: int32 [8], replicated, may hold values 0 or 1
Outputs:
- direction: float32 [8, 1024, 1024], P('dp', 'fsdp')
- first_next: float32 [8, 1024, 1024], P('dp', 'fsdp')
- second_next: float32 [8, 1024, 1024], P('dp', 'fsdp')
- gram_left: float32 [8, 1024, 1024], P('dp', 'fsdp')
- gram_right: float32 [8, 1024, 1024], P('dp', 'fsdp')
- basis_left: float32 [8, 1024, 1024], P('dp', 'fsdp')
- basis_right: float32 [8, 1024, 1024], P('dp', 'fsdp')
The draws below stay inside these ranges and needn't reach their ends.
All inputs are finite; a program needn't handle non-finite values.
Results may differ from the reference program's by a relative error of at most 0.0003.
Values sent between devices are 32-bit elements; how exact they have to be, the bound alone decides.
No kernel may reach another device: no remote copies, remote signals or barrier semaphores. Data moves between devices by JAX's collectives and lax.ppermute only.
A program may use at most 128 MiB of HBM per device.

```python
import math
import jax
import jax.numpy as jnp
from jax import lax

B = 1024
BLOCKS = 8
N_DP = 8


def symmetric_gram(key, top):
    diag_key, off_key = jax.random.split(key)
    diagonal = jax.random.uniform(diag_key, (BLOCKS, B), jnp.float32, 1.0, top)
    raw = jax.random.uniform(off_key, (BLOCKS, B, B), jnp.float32, -1.7320508, 1.7320508)
    off = (raw + jnp.swapaxes(raw, 1, 2)) * (0.3 / jnp.sqrt(2.0 * B))
    return off + diagonal[:, :, None] * jnp.eye(B, dtype=jnp.float32)[None]


def near_identity(key, spread):
    raw = jax.random.uniform(key, (BLOCKS, B, B), jnp.float32, -1.7320508, 1.7320508)
    return jnp.eye(B, dtype=jnp.float32)[None] + raw * (spread / jnp.sqrt(1.0 * B))


def draw_left_gram(key, part):
    key = jax.random.fold_in(key, 11)
    top = 2.0
    return symmetric_gram(key, top)


def draw_right_gram(key, part):
    key = jax.random.fold_in(key, 12)
    top = 2.0
    return symmetric_gram(key, top)


def draw_left_basis(key, part):
    key = jax.random.fold_in(key, 13)
    spread = 0.25
    return near_identity(key, spread)


def draw_right_basis(key, part):
    key = jax.random.fold_in(key, 14)
    spread = 0.25
    return near_identity(key, spread)


def place_ends(values, own_key, smallest, largest):
    longest = values.shape.index(max(values.shape))
    spots = []
    for shift in (0, 1):
        where = [jax.random.randint(jax.random.fold_in(own_key, axis), (), 0, length) for axis, length in enumerate(values.shape)]
        where[longest] = (where[longest] + shift) % values.shape[longest]
        spots.append(tuple(where))
    return values.at[spots[0]].set(smallest).at[spots[1]].set(largest)


def raised(drawn, stream_key, source, target, parts, factor):
    def block_of(dim):
        return (jnp.arange(drawn.shape[dim]) // (drawn.shape[dim] // parts)).reshape((-1,) + (1,) * (drawn.ndim - 1 - dim))

    first = jax.random.permutation(stream_key, parts)[block_of(target)]
    second = (block_of(target) + parts // 2) % parts
    return jnp.where((block_of(source) == first) | (block_of(source) == second), factor * drawn, drawn)


def steps_of(key, shape, cuts, least, high):
    def one(dim, shards_of):
        heights = jax.random.uniform(jax.random.fold_in(jax.random.fold_in(key, 6), dim), (shards_of,), jnp.float32, least / len(cuts), high / len(cuts))
        return jnp.repeat(jnp.exp(heights), shape[dim] // shards_of).reshape((-1,) + (1,) * (len(shape) - dim - 1))

    loudness = one(*cuts[0])
    for cut in cuts[1:]:
        loudness = loudness * one(*cut)
    return loudness


def bell_draw(stream_key, shape, scale, reach, shards=(), held_as=jnp.bfloat16):
    drawn = scale * jax.random.normal(stream_key, shape, jnp.float32)
    if shards:
        drawn = drawn * steps_of(stream_key, shape, shards, -0.22, 0.18)
    return jnp.clip(drawn, -reach, reach).astype(held_as)


def heavy_noise(stream_key, shape, scale, reach, shards, heavy, kind=jnp.bfloat16):
    array = scale * jax.random.normal(stream_key, shape, jnp.float32)
    if shards:
        array = array * steps_of(stream_key, shape, shards, -0.22, 0.18)
    return jnp.clip(raised(array, jax.random.fold_in(stream_key, 3), *heavy), -reach, reach).astype(kind)


def setup_inputs(seed: int = 0) -> dict:
    keys = jax.random.split(jax.random.key(seed), 9)
    grad_parts = heavy_noise(keys[0], (BLOCKS, N_DP, B, B), 0.04, 0.875, ((1, 8), (2, 32)), (1, 0, 8, 2.0))
    first_moment = bell_draw(keys[1], (BLOCKS, B, B), 0.1, 1.5, ((0, 8), (1, 32)), jnp.float32)
    second_moment = jnp.clip(jnp.exp(math.log(0.02) - 2.30258502 * jax.random.uniform(keys[2], (BLOCKS, B, B), jnp.float32) ** steps_of(keys[2], (BLOCKS, B, B), ((0, 8), (1, 32)), -0.2, 0.2)), 0.002, 0.02)
    left_gram = draw_left_gram(jax.random.fold_in(keys[8], 71), 0)
    right_gram = draw_right_gram(jax.random.fold_in(keys[8], 71), 0)
    left_basis = draw_left_basis(jax.random.fold_in(keys[8], 71), 0)
    right_basis = draw_right_basis(jax.random.fold_in(keys[8], 71), 0)
    due_flags = place_ends((jax.random.randint(keys[7], (BLOCKS,), 0, 3) < 1).astype(jnp.int32), jax.random.fold_in(keys[7], 1), 0, 1)
    return {"grad_parts": grad_parts, "first_moment": first_moment, "second_moment": second_moment, "left_gram": left_gram, "right_gram": right_gram, "left_basis": left_basis, "right_basis": right_basis, "due_flags": due_flags}


def matmul(left, right):
    return jnp.dot(left.astype(jnp.float32), right.astype(jnp.float32), precision=lax.Precision.HIGHEST, preferred_element_type=jnp.float32)

def one_block(items):
    grad, first_moment, second_moment, left_gram, right_gram, left_basis, right_basis, due = items
    rotated = matmul(matmul(left_basis.T, grad), right_basis)
    first_next = 0.9 * first_moment + 0.1 * rotated
    second_next = 0.95 * second_moment + 0.05 * rotated * rotated
    normed = first_next / (jnp.sqrt(second_next) + 1e-08)
    direction = matmul(left_basis, matmul(normed, right_basis.T))
    gram_left = 0.95 * left_gram + 0.05 * matmul(grad, grad.T)
    gram_right = 0.95 * right_gram + 0.05 * matmul(grad.T, grad)
    power_left = matmul(gram_left, left_basis)
    power_right = matmul(gram_right, right_basis)
    factor_left = jnp.linalg.cholesky(matmul(power_left.T, power_left))
    factor_right = jnp.linalg.cholesky(matmul(power_right.T, power_right))
    fresh_left = lax.linalg.triangular_solve(factor_left, power_left, left_side=False, lower=True, transpose_a=True)
    fresh_right = lax.linalg.triangular_solve(factor_right, power_right, left_side=False, lower=True, transpose_a=True)
    basis_left = jnp.where(due > 0, fresh_left, left_basis)
    basis_right = jnp.where(due > 0, fresh_right, right_basis)
    return (direction, first_next, second_next, gram_left, gram_right, basis_left, basis_right)

def reference(grad_parts, first_moment, second_moment, left_gram, right_gram, left_basis, right_basis, due_flags):
    grad = lax.optimization_barrier(jnp.sum(grad_parts.astype(jnp.float32), axis=1))
    outputs = lax.map(one_block, (grad, first_moment, second_moment, left_gram, right_gram, left_basis, right_basis, due_flags))
    return (outputs[0], outputs[1], outputs[2], outputs[3], outputs[4], outputs[5], outputs[6])
```

```python
import jax
import jax.numpy as jnp
from jax import lax
from jax.experimental import pallas as pl
from jax.experimental.pallas import tpu as pltpu
from jax.sharding import Mesh, PartitionSpec as P

N = 1024
NB = 128
GROUP = 2
ROWS = 32


def matmul(left, right, dims=((1,), (0,))):
    return lax.dot_general(
        left, right, (dims, ((), ())), precision=lax.Precision.HIGH, preferred_element_type=jnp.float32
    )


def split(values):
    high = values.astype(jnp.bfloat16)
    return high, (values - high.astype(jnp.float32)).astype(jnp.bfloat16)


def dot_split(a, b, contracted):
    dims = (((1,), (contracted,)), ((), ()))

    def one(u, v):
        return lax.dot_general(u, v, dims, preferred_element_type=jnp.float32)

    return one(a[0], b[0]) + (one(a[0], b[1]) + one(a[1], b[0]))


def dot_nt(a, b):
    return dot_split(a, b, 1)


def dot_nn(a, b):
    return dot_split(a, b, 0)


def inverse_factor(block):
    width = 8 * GROUP
    tiles = NB // 8
    rows = [block[8 * t : 8 * t + 8, :] for t in range(tiles)]
    lane = lax.broadcasted_iota(jnp.int32, (8, NB), 1)
    sub = lax.broadcasted_iota(jnp.int32, (8, NB), 0)

    def over_lanes(tile, column):
        return jnp.broadcast_to(tile[:, column : column + 1], (8, NB))

    def over_rows(tile, row):
        return jnp.broadcast_to(tile[row : row + 1, :], (8, NB))

    out = []
    for first in range(0, tiles, GROUP):
        start = 8 * first
        columns = [[over_lanes(rows[first + q], start + c) for q in range(GROUP)] for c in range(width)]
        inside = (lane >= start) & (lane < start + width)
        pivots = [
            jnp.where(inside, jnp.where(lane == sub + (start + 8 * q), 1.0, 0.0), rows[first + q])
            for q in range(GROUP)
        ]
        factor_rows = [None] * GROUP
        for j in range(width):
            own, s = divmod(j, 8)
            here = sub == s
            pivot = over_rows(columns[j][own], s)
            inverse = 1.0 / pivot
            row = over_rows(pivots[own], s)
            scaled = row * lax.rsqrt(pivot)
            factor_rows[own] = scaled if s == 0 else jnp.where(here, scaled, factor_rows[own])
            weights = [columns[j][q] * inverse for q in range(GROUP)]
            for q in range(GROUP):
                reduced = pivots[q] - weights[q] * row
                pivots[q] = jnp.where(here, row * inverse, reduced) if q == own else reduced
            for c in range(j + 1, width):
                across = over_rows(columns[c][own], s)
                for q in range(GROUP):
                    reduced = columns[c][q] - weights[q] * across
                    columns[c][q] = jnp.where(here, across * inverse, reduced) if q == own else reduced
        for q in range(GROUP):
            out.append(jnp.where(lane <= sub + (start + 8 * q), factor_rows[q], 0.0))
        if first + GROUP < tiles:
            solved = [over_rows(pivots[c // 8], c % 8) for c in range(width)]
            for t in range(first + GROUP, tiles):
                terms = [over_lanes(rows[t], start + c) * solved[c] for c in range(width)]
                while len(terms) > 1:
                    terms = [terms[i] + terms[i + 1] for i in range(0, len(terms), 2)]
                rows[t] = jnp.where(inside, 0.0, rows[t]) - terms[0]
    return jnp.concatenate(out, 0)


def rotate_kernel(
    place_ref, own_ref, other_ref, sides_ref, swapped_ref, moment_ref,
    ghigh, glow, bhigh, blow, moved_ref, projected_ref, grad_ref,
):
    z, core, side = place_ref[0], place_ref[1], place_ref[2]
    half = N // 2
    for t in range(8):
        for low in range(2):
            row = low * 256 + t * ROWS
            mine = pl.ds(pl.multiple_of(core * half + row, ROWS), ROWS)
            theirs = pl.ds(pl.multiple_of((1 - core) * half + row, ROWS), ROWS)
            bhigh[mine, :], blow[mine, :] = split(sides_ref[t, low])
            bhigh[theirs, :], blow[theirs, :] = split(swapped_ref[t, low])
    for ref, c in ((own_ref, core), (other_ref, 1 - core)):
        for low in range(2):
            for k in range(8):
                source = lax.rem(z + (8 - k), 8)
                at = pl.multiple_of(c * half + low * 256 + source * ROWS, ROWS)
                grad_ref[pl.ds(at, ROWS), :] = ref[low, k]

    @pl.when(side == 0)
    def _():
        for k in range(N // NB):
            at = pl.ds(k * NB, NB)
            ghigh[at, :], glow[at, :] = split(grad_ref[at, :])
        moved_ref[...] = jnp.zeros_like(moved_ref)
        projected_ref[...] = jnp.zeros_like(projected_ref)

    @pl.when(side == 1)
    def _():
        for k in range(N // NB):
            at = pl.ds(k * NB, NB)
            ghigh[at, :], glow[at, :] = split(grad_ref[:, at].T)
        basis = (bhigh[...], blow[...])
        turned = dot_nt(split(moment_ref[3]), (ghigh[...], glow[...]))
        rotated = dot_nn(split(turned), basis)
        first_next = 0.9 * moment_ref[0] + 0.1 * rotated
        second_next = 0.95 * moment_ref[1] + 0.05 * rotated * rotated
        normed = first_next / (jnp.sqrt(second_next) + 1e-08)
        moved_ref[0] = first_next
        moved_ref[1] = second_next
        projected_ref[...] = dot_nt(split(normed), basis)


def rotate(place, own, other, sides, swapped, moments):
    vmem = pl.BlockSpec(memory_space=pltpu.VMEM)
    shape = jax.ShapeDtypeStruct
    return pl.pallas_call(
        rotate_kernel,
        out_shape=(shape((N, N), jnp.bfloat16),) * 4
        + (shape((2, 2 * ROWS, N), jnp.float32), shape((2 * ROWS, N), jnp.float32)),
        in_specs=[pl.BlockSpec(memory_space=pltpu.SMEM)] + [vmem] * 5,
        out_specs=(vmem,) * 6,
        scratch_shapes=[pltpu.VMEM((N, N), jnp.float32)],
        compiler_params=pltpu.CompilerParams(vmem_limit_bytes=40 * 2**20),
        cost_estimate=pl.CostEstimate(flops=6 * 10**9, bytes_accessed=18 * 2**20, transcendentals=0),
        name="rotate",
    )(place, own, other, sides, swapped, moments)


def product_kernel(place_ref, ghigh, glow, bhigh, blow, sides_ref, power_ref, gram_ref, ahigh, alow):
    z, core = place_ref[0], place_ref[1]
    half = N // 2
    grad = (ghigh[...], glow[...])
    for piece in range(4):
        low, first = divmod(piece, 2)
        at = pl.ds(pl.multiple_of(core * half + piece * NB, NB), NB)
        outer = dot_nt((ghigh[at, :], glow[at, :]), grad)
        for t in range(4):
            new = 0.95 * sides_ref[first * 4 + t, 2 + low] + 0.05 * outer[t * ROWS : (t + 1) * ROWS, :]
            power_ref[pl.ds(piece * NB + t * ROWS, ROWS), :] = new
    for low in range(2):
        gram_ref[pl.ds(low * ROWS, ROWS), :] = power_ref[pl.ds(pl.multiple_of(low * 256 + z * ROWS, ROWS), ROWS), :]
    ahigh[...], alow[...] = split(power_ref[...])
    power_ref[...] = dot_nn((ahigh[...], alow[...]), (bhigh[...], blow[...]))


def products(place, ghigh, glow, bhigh, blow, sides):
    vmem = pl.BlockSpec(memory_space=pltpu.VMEM)
    shape = jax.ShapeDtypeStruct
    half = pltpu.VMEM((N // 2, N), jnp.bfloat16)
    return pl.pallas_call(
        product_kernel,
        out_shape=(shape((N // 2, N), jnp.float32), shape((2 * ROWS, N), jnp.float32)),
        in_specs=[pl.BlockSpec(memory_space=pltpu.SMEM)] + [vmem] * 5,
        out_specs=(vmem,) * 2,
        scratch_shapes=[half, half],
        compiler_params=pltpu.CompilerParams(vmem_limit_bytes=40 * 2**20),
        cost_estimate=pl.CostEstimate(flops=8 * 10**9, bytes_accessed=14 * 2**20, transcendentals=0),
        name="products",
    )(place, ghigh, glow, bhigh, blow, sides)


def factor_kernel(place_ref, own_ref, other_ref, out_ref, work, high, low):
    z = place_ref[0]
    half = N // 2
    mine = 2 * ROWS
    for k in range(N // NB):
        this = pl.ds(k * NB, NB)
        for at, ref in ((0, own_ref), (half, other_ref)):
            high[this, pl.ds(at, half)], low[this, pl.ds(at, half)] = split(ref[:, this].T)
    for k in range(N // NB):
        below = pl.ds(k * NB, N - k * NB)
        this = pl.ds(k * NB, NB)
        work[below, this] = dot_nt((high[below, :], low[below, :]), (high[this, :], low[this, :]))
    for t in range(2):
        work[pl.ds(N + t * ROWS, ROWS), :] = own_ref[pl.ds(pl.multiple_of(t * 256 + z * ROWS, ROWS), ROWS), :]
    for k in range(N // NB):
        this = pl.ds(k * NB, NB)
        after = (k + 1) * NB
        left = N - after
        inverse = inverse_factor(work[this, this])
        panel = dot_nt(split(work[pl.ds(after, left + mine), this]), split(inverse))
        out_ref[:, this] = panel[left:, :]
        if left:
            parts = split(panel)
            upper = (parts[0][:left], parts[1][:left])
            work[pl.ds(after, left + mine), pl.ds(after, NB)] -= dot_nt(parts, (upper[0][:NB], upper[1][:NB]))
            if left > NB:
                rest = after + NB
                work[pl.ds(rest, left + mine - NB), pl.ds(rest, left - NB)] -= dot_nt(
                    (parts[0][NB:], parts[1][NB:]), (upper[0][NB:], upper[1][NB:])
                )


def orthogonal_rows(place, own, other):
    vmem = pl.BlockSpec(memory_space=pltpu.VMEM)
    rows = 2 * ROWS
    return pl.pallas_call(
        factor_kernel,
        out_shape=jax.ShapeDtypeStruct((rows, N), jnp.float32),
        in_specs=[pl.BlockSpec(memory_space=pltpu.SMEM), vmem, vmem],
        out_specs=vmem,
        scratch_shapes=[
            pltpu.VMEM((N + rows, N), jnp.float32),
            pltpu.VMEM((N, N), jnp.bfloat16),
            pltpu.VMEM((N, N), jnp.bfloat16),
        ],
        compiler_params=pltpu.CompilerParams(vmem_limit_bytes=48 * 2**20),
        cost_estimate=pl.CostEstimate(flops=40 * 10**9, bytes_accessed=5 * 2**20, transcendentals=0),
        name="factor",
    )(place, own, other)


def shift(size, step):
    return [(i, (i + step) % size) for i in range(size)]


def owner_routes():
    first, second = [], []
    for core in range(2):
        for y in range(4):
            source, left = core * 4 + y, (y // 2) * 4 + 2 * core
            (first if y % 2 == 0 else second).append((source, left))
            (second if y % 2 == 0 else first).append((source, left + 1))
    return first, second


def shards(grad_parts, first_moment, second_moment, left_gram, right_gram, left_basis, right_basis, due_flags):
    x, core, y, z = (lax.axis_index(name) for name in ("x", "core", "y", "z"))
    even = y % 2 == 0
    route_a, route_b = owner_routes()
    pair = ("core", "y")

    def to_chains(for_left, for_right):
        got_a = lax.ppermute(jnp.where(even, for_left, for_right), pair, route_a)
        got_b = lax.ppermute(jnp.where(even, for_right, for_left), pair, route_b)
        return jnp.where(even, got_a, got_b), jnp.where(even, got_b, got_a)

    def to_owners(low, high):
        got_a = lax.ppermute(jnp.where(even, low, high), pair, [(d, s) for s, d in route_a])
        got_b = lax.ppermute(jnp.where(even, high, low), pair, [(d, s) for s, d in route_b])
        return jnp.where(even, got_a, got_b), jnp.where(even, got_b, got_a)

    parts = grad_parts.reshape(4, 2, ROWS, N)
    kept = lax.dynamic_index_in_dim(parts, core, 1, keepdims=False).astype(jnp.float32)
    given = lax.dynamic_index_in_dim(parts, 1 - core, 1, keepdims=False).astype(jnp.float32)
    halves = kept + lax.ppermute(given, "core", shift(2, 1))
    sides = (jnp.concatenate([left_basis, left_gram]), jnp.concatenate([right_basis, right_gram]))
    halves, sides = lax.optimization_barrier((halves, sides))
    low, high = to_chains(*sides)
    total = lax.dynamic_index_in_dim(halves, x, 0, keepdims=False)
    for step in (1, 2, 3):
        sent = lax.dynamic_index_in_dim(halves, (x + step) % 4, 0, keepdims=False)
        total = total + lax.ppermute(sent, "x", shift(4, step))

    rows = jnp.concatenate([jnp.stack([low[0], high[0]]), jnp.stack([low[1], high[1]])])
    sides = lax.all_gather(rows, "z", axis=0, tiled=False)

    low, high = to_chains(total, total)
    rows = jnp.concatenate([low, high])
    pieces = {0: rows}
    up, down = lax.ppermute(rows, "z", shift(8, 1)), lax.ppermute(rows, "z", shift(8, -1))
    pieces[1], pieces[7] = up, down
    mine, total = lax.optimization_barrier((left_basis[0], total))
    tiles = mine.reshape(ROWS, 32, ROWS).transpose(1, 2, 0).reshape(32, 8, 128)
    tiles = lax.all_to_all(tiles, ("y", "z"), 0, 0, tiled=True)
    columns = tiles.reshape(32, ROWS, ROWS).transpose(1, 0, 2).reshape(ROWS, N)
    moments = jnp.stack([first_moment[0], second_moment[0], left_basis[0], columns])
    to_right = [[(c * 4 + y0, (y0 // 2) * 4 + 2 * c + 1) for c in (0, 1) for y0 in (odd, odd + 2)] for odd in (0, 1)]
    low, high = (lax.ppermute(moments, pair, route) for route in to_right)
    moments = jnp.concatenate([low, high], axis=1)
    up, down = lax.ppermute(up, "z", shift(8, 1)), lax.ppermute(down, "z", shift(8, -1))
    up, down, moments = lax.optimization_barrier((up, down, moments))
    pieces[2], pieces[6] = up, down
    up, down = lax.ppermute(up, "z", shift(8, 1)), lax.ppermute(down, "z", shift(8, -1))
    pieces[3], pieces[5] = up, down
    up = lax.ppermute(up[:ROWS], "z", shift(8, 1))
    down = lax.ppermute(down[ROWS:], "z", shift(8, -1))
    low = [pieces[k][:ROWS] for k in range(4)] + [up] + [pieces[k][:ROWS] for k in (5, 6, 7)]
    high = [pieces[k][ROWS:] for k in range(4)] + [down] + [pieces[k][ROWS:] for k in (5, 6, 7)]
    own = jnp.stack([jnp.stack(low), jnp.stack(high)])
    other = lax.ppermute(own, "core", shift(2, 1))
    swapped = lax.ppermute(sides[:, :2], "core", shift(2, 1))

    place = jnp.stack([z, core, y % 2]).astype(jnp.int32)
    *operands, moved, projected = rotate(place, own, other, sides, swapped, moments)
    projected = lax.all_gather(projected, ("core", "z"), axis=0, tiled=True)
    back = [[(d, source) for source, d in route] for route in to_right]
    moved_low = lax.ppermute(moved[:, :ROWS], pair, back[0])
    moved_high = lax.ppermute(moved[:, ROWS:], pair, back[1])
    power, new_gram = products(place, *operands, sides)
    fresh = orthogonal_rows(place, power, lax.ppermute(power, "core", shift(2, 1)))
    projected = projected.reshape(2, 8, 2, ROWS, N).transpose(0, 2, 1, 3, 4).reshape(N, N)
    direction = matmul(moments[2], projected)

    late = jnp.stack([fresh, direction, new_gram])
    late_left, late_right = to_owners(late[:, :ROWS], late[:, ROWS:])
    moved = jnp.where(even, moved_low, moved_high)
    due = lax.dynamic_index_in_dim(due_flags, 2 * x + core, 0, keepdims=False) > 0
    return (
        late_right[1][None],
        moved[0][None],
        moved[1][None],
        late_left[2][None],
        late_right[2][None],
        jnp.where(due, late_left[:1], left_basis),
        jnp.where(due, late_right[:1], right_basis),
    )


def solution(mesh):
    whole = Mesh(mesh.devices.reshape(4, 2, 4, 8), ("x", "core", "y", "z"))
    rows = P(("x", "core"), ("y", "z"), None)
    return jax.shard_map(
        shards,
        mesh=whole,
        in_specs=(P(None, ("x", "core"), ("y", "z"), None), rows, rows, rows, rows, rows, rows, P()),
        out_specs=(rows,) * 7,
        check_vma=False,
    )
```

```python
import jax
import jax.numpy as jnp
from jax import lax
from jax.experimental import pallas as pl
from jax.experimental.pallas import tpu as pltpu
from jax.sharding import Mesh, PartitionSpec as P

N = 1024
NB = 128
GROUP = 2
ROWS = 32


def matmul(left, right, dims=((1,), (0,))):
    return lax.dot_general(
        left, right, (dims, ((), ())), precision=lax.Precision.HIGH, preferred_element_type=jnp.float32
    )


def split(values):
    high = values.astype(jnp.bfloat16)
    return high, (values - high.astype(jnp.float32)).astype(jnp.bfloat16)


def dot_split(a, b, contracted):
    dims = (((1,), (contracted,)), ((), ()))

    def one(u, v):
        return lax.dot_general(u, v, dims, preferred_element_type=jnp.float32)

    return one(a[0], b[0]) + (one(a[0], b[1]) + one(a[1], b[0]))


def dot_nt(a, b):
    return dot_split(a, b, 1)


def dot_nn(a, b):
    return dot_split(a, b, 0)


def inverse_factor(block):
    width = 8 * GROUP
    tiles = NB // 8
    rows = [block[8 * t : 8 * t + 8, :] for t in range(tiles)]
    lane = lax.broadcasted_iota(jnp.int32, (8, NB), 1)
    sub = lax.broadcasted_iota(jnp.int32, (8, NB), 0)

    def over_lanes(tile, column):
        return jnp.broadcast_to(tile[:, column : column + 1], (8, NB))

    def over_rows(tile, row):
        return jnp.broadcast_to(tile[row : row + 1, :], (8, NB))

    out = []
    for first in range(0, tiles, GROUP):
        start = 8 * first
        columns = [[over_lanes(rows[first + q], start + c) for q in range(GROUP)] for c in range(width)]
        inside = (lane >= start) & (lane < start + width)
        pivots = [
            jnp.where(inside, jnp.where(lane == sub + (start + 8 * q), 1.0, 0.0), rows[first + q])
            for q in range(GROUP)
        ]
        factor_rows = [None] * GROUP
        for j in range(width):
            own, s = divmod(j, 8)
            here = sub == s
            pivot = over_rows(columns[j][own], s)
            inverse = 1.0 / pivot
            row = over_rows(pivots[own], s)
            scaled = row * lax.rsqrt(pivot)
            factor_rows[own] = scaled if s == 0 else jnp.where(here, scaled, factor_rows[own])
            weights = [columns[j][q] * inverse for q in range(GROUP)]
            for q in range(GROUP):
                reduced = pivots[q] - weights[q] * row
                pivots[q] = jnp.where(here, row * inverse, reduced) if q == own else reduced
            for c in range(j + 1, width):
                across = over_rows(columns[c][own], s)
                for q in range(GROUP):
                    reduced = columns[c][q] - weights[q] * across
                    columns[c][q] = jnp.where(here, across * inverse, reduced) if q == own else reduced
        for q in range(GROUP):
            out.append(jnp.where(lane <= sub + (start + 8 * q), factor_rows[q], 0.0))
        if first + GROUP < tiles:
            solved = [over_rows(pivots[c // 8], c % 8) for c in range(width)]
            for t in range(first + GROUP, tiles):
                terms = [over_lanes(rows[t], start + c) * solved[c] for c in range(width)]
                while len(terms) > 1:
                    terms = [terms[i] + terms[i + 1] for i in range(0, len(terms), 2)]
                rows[t] = jnp.where(inside, 0.0, rows[t]) - terms[0]
    return jnp.concatenate(out, 0)


def assemble(place_ref, own_ref, other_ref, sides_ref, swapped_ref, ghigh, glow, bhigh, blow, grad_ref):
    z, core, side = place_ref[0], place_ref[1], place_ref[2]
    half = N // 2
    for t in range(8):
        for low in range(2):
            row = low * 256 + t * ROWS
            mine = pl.ds(pl.multiple_of(core * half + row, ROWS), ROWS)
            theirs = pl.ds(pl.multiple_of((1 - core) * half + row, ROWS), ROWS)
            bhigh[mine, :], blow[mine, :] = split(sides_ref[t, low])
            bhigh[theirs, :], blow[theirs, :] = split(swapped_ref[t, low])
    for ref, c in ((own_ref, core), (other_ref, 1 - core)):
        for low in range(2):
            for k in range(8):
                source = lax.rem(z + (8 - k), 8)
                at = pl.multiple_of(c * half + low * 256 + source * ROWS, ROWS)
                grad_ref[pl.ds(at, ROWS), :] = ref[low, k]

    @pl.when(side == 0)
    def _():
        for k in range(N // NB):
            at = pl.ds(k * NB, NB)
            ghigh[at, :], glow[at, :] = split(grad_ref[at, :])

    @pl.when(side == 1)
    def _():
        for k in range(N // NB):
            at = pl.ds(k * NB, NB)
            ghigh[at, :], glow[at, :] = split(grad_ref[:, at].T)


def rotate_kernel(
    place_ref, own_ref, other_ref, sides_ref, swapped_ref, moment_ref,
    moved_ref, projected_ref, ghigh, glow, bhigh, blow, grad_ref,
):
    side = place_ref[2]

    @pl.when(side == 0)
    def _():
        moved_ref[...] = jnp.zeros_like(moved_ref)
        projected_ref[...] = jnp.zeros_like(projected_ref)

    @pl.when(side == 1)
    def _():
        assemble(place_ref, own_ref, other_ref, sides_ref, swapped_ref, ghigh, glow, bhigh, blow, grad_ref)
        basis = (bhigh[...], blow[...])
        turned = dot_nt(split(moment_ref[3]), (ghigh[...], glow[...]))
        rotated = dot_nn(split(turned), basis)
        first_next = 0.9 * moment_ref[0] + 0.1 * rotated
        second_next = 0.95 * moment_ref[1] + 0.05 * rotated * rotated
        normed = first_next / (jnp.sqrt(second_next) + 1e-08)
        moved_ref[0] = first_next
        moved_ref[1] = second_next
        projected_ref[...] = dot_nt(split(normed), basis)


def rotate(place, own, other, sides, swapped, moments):
    vmem = pl.BlockSpec(memory_space=pltpu.VMEM)
    shape = jax.ShapeDtypeStruct
    return pl.pallas_call(
        rotate_kernel,
        out_shape=(shape((2, 2 * ROWS, N), jnp.float32), shape((2 * ROWS, N), jnp.float32)),
        in_specs=[pl.BlockSpec(memory_space=pltpu.SMEM)] + [vmem] * 5,
        out_specs=(vmem,) * 2,
        scratch_shapes=[pltpu.VMEM((N, N), jnp.bfloat16)] * 4 + [pltpu.VMEM((N, N), jnp.float32)],
        compiler_params=pltpu.CompilerParams(vmem_limit_bytes=40 * 2**20),
        cost_estimate=pl.CostEstimate(flops=6 * 10**9, bytes_accessed=18 * 2**20, transcendentals=0),
        name="rotate",
    )(place, own, other, sides, swapped, moments)


def product_kernel(
    place_ref, own_ref, other_ref, sides_ref, swapped_ref,
    power_ref, gram_ref, ahigh, alow, ghigh, glow, bhigh, blow, grad_ref,
):
    z, core = place_ref[0], place_ref[1]
    half = N // 2
    assemble(place_ref, own_ref, other_ref, sides_ref, swapped_ref, ghigh, glow, bhigh, blow, grad_ref)
    grad = (ghigh[...], glow[...])
    for piece in range(4):
        low, first = divmod(piece, 2)
        at = pl.ds(pl.multiple_of(core * half + piece * NB, NB), NB)
        outer = dot_nt((ghigh[at, :], glow[at, :]), grad)
        for t in range(4):
            new = 0.95 * sides_ref[first * 4 + t, 2 + low] + 0.05 * outer[t * ROWS : (t + 1) * ROWS, :]
            power_ref[pl.ds(piece * NB + t * ROWS, ROWS), :] = new
    for low in range(2):
        gram_ref[pl.ds(low * ROWS, ROWS), :] = power_ref[pl.ds(pl.multiple_of(low * 256 + z * ROWS, ROWS), ROWS), :]
    ahigh[...], alow[...] = split(power_ref[...])
    power_ref[...] = dot_nn((ahigh[...], alow[...]), (bhigh[...], blow[...]))


def products(place, own, other, sides, swapped):
    vmem = pl.BlockSpec(memory_space=pltpu.VMEM)
    shape = jax.ShapeDtypeStruct
    half = pltpu.VMEM((N // 2, N), jnp.bfloat16)
    return pl.pallas_call(
        product_kernel,
        out_shape=(shape((N // 2, N), jnp.float32), shape((2 * ROWS, N), jnp.float32)),
        in_specs=[pl.BlockSpec(memory_space=pltpu.SMEM)] + [vmem] * 4,
        out_specs=(vmem,) * 2,
        scratch_shapes=[half, half] + [pltpu.VMEM((N, N), jnp.bfloat16)] * 4 + [pltpu.VMEM((N, N), jnp.float32)],
        compiler_params=pltpu.CompilerParams(vmem_limit_bytes=40 * 2**20),
        cost_estimate=pl.CostEstimate(flops=8 * 10**9, bytes_accessed=14 * 2**20, transcendentals=0),
        name="products",
    )(place, own, other, sides, swapped)


def factor_kernel(place_ref, own_ref, other_ref, out_ref, work, high, low):
    z = place_ref[0]
    half = N // 2
    mine = 2 * ROWS
    for k in range(N // NB):
        this = pl.ds(k * NB, NB)
        for at, ref in ((0, own_ref), (half, other_ref)):
            high[this, pl.ds(at, half)], low[this, pl.ds(at, half)] = split(ref[:, this].T)
    for k in range(N // NB):
        below = pl.ds(k * NB, N - k * NB)
        this = pl.ds(k * NB, NB)
        work[below, this] = dot_nt((high[below, :], low[below, :]), (high[this, :], low[this, :]))
    for t in range(2):
        work[pl.ds(N + t * ROWS, ROWS), :] = own_ref[pl.ds(pl.multiple_of(t * 256 + z * ROWS, ROWS), ROWS), :]
    for k in range(N // NB):
        this = pl.ds(k * NB, NB)
        after = (k + 1) * NB
        left = N - after
        inverse = inverse_factor(work[this, this])
        panel = dot_nt(split(work[pl.ds(after, left + mine), this]), split(inverse))
        out_ref[:, this] = panel[left:, :]
        if left:
            parts = split(panel)
            upper = (parts[0][:left], parts[1][:left])
            work[pl.ds(after, left + mine), pl.ds(after, NB)] -= dot_nt(parts, (upper[0][:NB], upper[1][:NB]))
            if left > NB:
                rest = after + NB
                work[pl.ds(rest, left + mine - NB), pl.ds(rest, left - NB)] -= dot_nt(
                    (parts[0][NB:], parts[1][NB:]), (upper[0][NB:], upper[1][NB:])
                )


def orthogonal_rows(place, own, other):
    vmem = pl.BlockSpec(memory_space=pltpu.VMEM)
    rows = 2 * ROWS
    return pl.pallas_call(
        factor_kernel,
        out_shape=jax.ShapeDtypeStruct((rows, N), jnp.float32),
        in_specs=[pl.BlockSpec(memory_space=pltpu.SMEM), vmem, vmem],
        out_specs=vmem,
        scratch_shapes=[
            pltpu.VMEM((N + rows, N), jnp.float32),
            pltpu.VMEM((N, N), jnp.bfloat16),
            pltpu.VMEM((N, N), jnp.bfloat16),
        ],
        compiler_params=pltpu.CompilerParams(vmem_limit_bytes=48 * 2**20),
        cost_estimate=pl.CostEstimate(flops=40 * 10**9, bytes_accessed=5 * 2**20, transcendentals=0),
        name="factor",
    )(place, own, other)


def shift(size, step):
    return [(i, (i + step) % size) for i in range(size)]


def owner_routes():
    first, second = [], []
    for core in range(2):
        for y in range(4):
            source, left = core * 4 + y, (y // 2) * 4 + 2 * core
            (first if y % 2 == 0 else second).append((source, left))
            (second if y % 2 == 0 else first).append((source, left + 1))
    return first, second


def shards(grad_parts, first_moment, second_moment, left_gram, right_gram, left_basis, right_basis, due_flags):
    x, core, y, z = (lax.axis_index(name) for name in ("x", "core", "y", "z"))
    even = y % 2 == 0
    route_a, route_b = owner_routes()
    pair = ("core", "y")

    def to_chains(for_left, for_right):
        got_a = lax.ppermute(jnp.where(even, for_left, for_right), pair, route_a)
        got_b = lax.ppermute(jnp.where(even, for_right, for_left), pair, route_b)
        return jnp.where(even, got_a, got_b), jnp.where(even, got_b, got_a)

    def to_owners(low, high):
        got_a = lax.ppermute(jnp.where(even, low, high), pair, [(d, s) for s, d in route_a])
        got_b = lax.ppermute(jnp.where(even, high, low), pair, [(d, s) for s, d in route_b])
        return jnp.where(even, got_a, got_b), jnp.where(even, got_b, got_a)

    parts = grad_parts.reshape(4, 2, ROWS, N)
    kept = lax.dynamic_index_in_dim(parts, core, 1, keepdims=False).astype(jnp.float32)
    given = lax.dynamic_index_in_dim(parts, 1 - core, 1, keepdims=False).astype(jnp.float32)
    halves = kept + lax.ppermute(given, "core", shift(2, 1))
    sides = (jnp.concatenate([left_basis, left_gram]), jnp.concatenate([right_basis, right_gram]))
    halves, sides = lax.optimization_barrier((halves, sides))
    low, high = to_chains(*sides)
    total = lax.dynamic_index_in_dim(halves, x, 0, keepdims=False)
    for step in (1, 2, 3):
        sent = lax.dynamic_index_in_dim(halves, (x + step) % 4, 0, keepdims=False)
        total = total + lax.ppermute(sent, "x", shift(4, step))

    rows = jnp.concatenate([jnp.stack([low[0], high[0]]), jnp.stack([low[1], high[1]])])
    sides = lax.all_gather(rows, "z", axis=0, tiled=False)

    low, high = to_chains(total, total)
    rows = jnp.concatenate([low, high])
    pieces = {0: rows}
    up, down = lax.ppermute(rows, "z", shift(8, 1)), lax.ppermute(rows, "z", shift(8, -1))
    pieces[1], pieces[7] = up, down
    mine, total = lax.optimization_barrier((left_basis[0], total))
    tiles = mine.reshape(ROWS, 32, ROWS).transpose(1, 2, 0).reshape(32, 8, 128)
    tiles = lax.all_to_all(tiles, ("y", "z"), 0, 0, tiled=True)
    columns = tiles.reshape(32, ROWS, ROWS).transpose(1, 0, 2).reshape(ROWS, N)
    moments = jnp.stack([first_moment[0], second_moment[0], left_basis[0], columns])
    to_right = [[(c * 4 + y0, (y0 // 2) * 4 + 2 * c + 1) for c in (0, 1) for y0 in (odd, odd + 2)] for odd in (0, 1)]
    low, high = (lax.ppermute(moments, pair, route) for route in to_right)
    moments = jnp.concatenate([low, high], axis=1)
    up, down = lax.ppermute(up, "z", shift(8, 1)), lax.ppermute(down, "z", shift(8, -1))
    up, down, moments = lax.optimization_barrier((up, down, moments))
    pieces[2], pieces[6] = up, down
    up, down = lax.ppermute(up, "z", shift(8, 1)), lax.ppermute(down, "z", shift(8, -1))
    pieces[3], pieces[5] = up, down
    up = lax.ppermute(up[:ROWS], "z", shift(8, 1))
    down = lax.ppermute(down[ROWS:], "z", shift(8, -1))
    low = [pieces[k][:ROWS] for k in range(4)] + [up] + [pieces[k][:ROWS] for k in (5, 6, 7)]
    high = [pieces[k][ROWS:] for k in range(4)] + [down] + [pieces[k][ROWS:] for k in (5, 6, 7)]
    own = jnp.stack([jnp.stack(low), jnp.stack(high)])
    other = lax.ppermute(own, "core", shift(2, 1))
    swapped = lax.ppermute(sides[:, :2], "core", shift(2, 1))

    place = jnp.stack([z, core, y % 2]).astype(jnp.int32)
    moved, projected = rotate(place, own, other, sides, swapped, moments)
    projected = lax.all_gather(projected, ("core", "z"), axis=0, tiled=True)
    back = [[(d, source) for source, d in route] for route in to_right]
    moved_low = lax.ppermute(moved[:, :ROWS], pair, back[0])
    moved_high = lax.ppermute(moved[:, ROWS:], pair, back[1])
    power, new_gram = products(place, own, other, sides, swapped)
    fresh = orthogonal_rows(place, power, lax.ppermute(power, "core", shift(2, 1)))
    projected = projected.reshape(2, 8, 2, ROWS, N).transpose(0, 2, 1, 3, 4).reshape(N, N)
    direction = matmul(moments[2], projected)

    late = jnp.stack([fresh, direction, new_gram])
    late_left, late_right = to_owners(late[:, :ROWS], late[:, ROWS:])
    moved = jnp.where(even, moved_low, moved_high)
    due = lax.dynamic_index_in_dim(due_flags, 2 * x + core, 0, keepdims=False) > 0
    return (
        late_right[1][None],
        moved[0][None],
        moved[1][None],
        late_left[2][None],
        late_right[2][None],
        jnp.where(due, late_left[:1], left_basis),
        jnp.where(due, late_right[:1], right_basis),
    )


def solution(mesh):
    whole = Mesh(mesh.devices.reshape(4, 2, 4, 8), ("x", "core", "y", "z"))
    rows = P(("x", "core"), ("y", "z"), None)
    return jax.shard_map(
        shards,
        mesh=whole,
        in_specs=(P(None, ("x", "core"), ("y", "z"), None), rows, rows, rows, rows, rows, rows, P()),
        out_specs=(rows,) * 7,
        check_vma=False,
    )
```
